32 devices in a mesh: idx: 8 (over z, y), tp: 4 (over x, core).
Axes of the slice: x: 2, y: 2, z: 4, core: 2. Of those that a mesh axis runs over, the one named last changes fastest.
Arguments:
- activations: bfloat16 [8192, 28672], P('idx', 'tp'), may hold values from -6 to 6
- out_grads: bfloat16 [8192, 8192], P('idx', 'tp'), may hold values from -6 to 6
- proj_in: bfloat16 [28672, 64], P('tp'), may hold values from -0.03125 to 0.03125
- proj_out: bfloat16 [8192, 64], P('tp'), may hold values from -0.0625 to 0.0625
- doc_ids: int32 [8192], P('idx'), may hold values from 0 to 1023, never falling along the last dimension, each value on 1 to 32 neighbouring positions
- doc_order: int32 [1024], replicated, may hold values from 0 to 1023, each once
- inv_fisher: float32 [4096, 4096], P('tp'), may hold values from -1 to 3, as said below
- index_grads: bfloat16 [32768, 4096], P(('idx', 'tp')), may hold values from -0.0234375 to 0.0234375
Outputs:
- scores: float32 [1024, 32768], P(None, ('idx', 'tp'))
The draws below stay inside these ranges and needn't reach their ends.
Inputs may be any that keep to these rules, and one draw needn't show every extreme that they name: `inv_fisher`: an estimate of the inverse Fisher of the projected gradients.
All inputs are finite; a program needn't handle non-finite values.
Results may differ from the reference program's by a relative error of at most 0.0029.
Values may be sent and summed in bfloat16 or wider, within the bound.
No kernel may reach another device: no remote copies, remote signals or barrier semaphores. Data moves between devices by JAX's collectives and lax.ppermute only.
A program may use at most 128 MiB of HBM per device.

```python
import math
import jax
import jax.numpy as jnp
import numpy as np
from jax import lax

D = 8192
FF = 28672
R = 64
NDOC = 1024
TOKENS = 8192
INDEXED = 32768
KDIM = 4096


def draw_inv_fisher(key, part):
    width = R * R
    first_key, second_key = jax.random.split(jax.random.fold_in(key, 11))
    diagonal = jnp.exp(jax.random.uniform(first_key, (width,), jnp.float32, jnp.log(0.5), jnp.log(2.0)))
    spread = jax.random.normal(second_key, (width, width), jnp.float32)
    spread = spread * (0.5 / jnp.sqrt(jnp.float32(width)))
    return ((spread + spread.T) * 0.70710678 + jnp.diag(diagonal)).astype(jnp.float32)


def shard_levels(key, extent, pieces, smallest, largest):
    level, own = 1.0, jax.random.fold_in(key, 6)
    for dim, parts in pieces:
        draws = jnp.exp(jax.random.uniform(jax.random.fold_in(own, dim), (parts,), jnp.float32, smallest / len(pieces), largest / len(pieces)))
        level = level * jnp.repeat(draws, extent[dim] // parts).reshape([-1 if axis == dim else 1 for axis in range(len(extent))])
    return level


def profile(number_of, total, limit, slope):
    weights = [(1 << 20) // math.isqrt(standing ** slope) + 1 for standing in range(2, number_of + 1)]
    surplus, given = total - limit - (number_of - 1), [1] * (number_of - 1)
    while surplus > 0:
        movable = [i for i in range(number_of - 1) if given[i] < limit]
        whole, budget = sum([weights[i] for i in movable]), surplus
        for i in movable:
            addition = min(limit - given[i], max(1, budget * weights[i] // whole), surplus)
            given[i] = given[i] + addition
            surplus = surplus - addition
    return np.array([limit] + given)


def ragged(key, count, total, most, lean):
    if count == 2:
        one = jax.random.randint(key, (), max(1, total - most), min(most, total - 1) + 1)
        return jnp.stack([one, total - one])
    sizes = jnp.asarray(profile(count, total, most, lean), jnp.int32)
    couples = (count - 1) // 2
    giver, taker = sizes[1:1 + 2 * couples:2], sizes[2:2 + 2 * couples:2]
    margin = jnp.minimum(giver - 1, most - taker)
    moved = jax.random.randint(jax.random.fold_in(key, 1), (couples,), 0, 1 << 20) % (margin + 1)
    sizes = sizes.at[1:1 + 2 * couples:2].set(giver - moved).at[2:2 + 2 * couples:2].set(taker + moved)
    return sizes[jax.random.permutation(jax.random.fold_in(key, 2), count)]


def centred(key, extent, scale, limit, cuts=(), dtype=jnp.bfloat16):
    drawn = jax.random.normal(key, extent, jnp.float32) * scale
    if len(cuts) > 0:
        drawn = shard_levels(key, extent, cuts, -0.22, 0.18) * drawn
    return jnp.clip(drawn, min=-limit, max=limit).astype(dtype)


def setup_inputs(seed: int = 0) -> dict:
    splits = jax.random.split(jax.random.key(seed), 9)
    activations = centred(splits[0], (TOKENS, FF), 1.0, 6.0, ((0, 8), (1, 4)))
    out_grads = centred(splits[1], (TOKENS, D), 1.0, 6.0, ((0, 8), (1, 4)))
    proj_in = centred(splits[2], (FF, R), FF ** -0.5, 0.03125, ((0, 4),))
    proj_out = centred(splits[3], (D, R), D ** -0.5, 0.0625, ((0, 4),))
    doc_ids = jnp.searchsorted(jnp.cumsum(ragged(splits[4], NDOC, TOKENS, 4 * TOKENS // NDOC, 1)), jnp.arange(TOKENS), side="right").astype(jnp.int32)
    doc_order = jax.random.permutation(splits[5], NDOC).astype(jnp.int32)
    inv_fisher = draw_inv_fisher(jax.random.fold_in(splits[8], 71), 0)
    index_grads = centred(splits[7], (INDEXED, KDIM), (16 * R * R) ** -0.5, 0.0234375, ((0, 32),))
    return dict(activations=activations, out_grads=out_grads, proj_in=proj_in, proj_out=proj_out, doc_ids=doc_ids, doc_order=doc_order, inv_fisher=inv_fisher, index_grads=index_grads)


def reference(activations, out_grads, proj_in, proj_out, doc_ids, doc_order, inv_fisher, index_grads):
    proj_acts = jnp.dot(activations, proj_in, preferred_element_type=jnp.float32)
    proj_grads = jnp.dot(out_grads, proj_out, preferred_element_type=jnp.float32)
    token_grads = (proj_grads[:, :, None] * proj_acts[:, None, :]).reshape(TOKENS, R * R)
    membership = (doc_ids[:, None] == doc_order[None, :]).astype(jnp.float32)
    doc_grads = lax.dot_general(membership, token_grads, (((0,), (0,)), ((), ())),
                                precision=lax.Precision.HIGHEST, preferred_element_type=jnp.float32)
    conditioned = jnp.dot(doc_grads, inv_fisher, precision=lax.Precision.HIGHEST,
                          preferred_element_type=jnp.float32)
    queries = conditioned.astype(jnp.bfloat16)
    return lax.dot_general(queries, index_grads, (((1,), (1,)), ((), ())),
                           preferred_element_type=jnp.float32)
```

```python
import jax
import jax.numpy as jnp
from jax import lax
from jax.experimental import pallas as pl
from jax.experimental.pallas import tpu as pltpu
from jax.sharding import PartitionSpec as P

HIGHEST = lax.Precision.HIGHEST
HIGH = lax.Precision.HIGH
AXES = ("idx", "tp")


def place_rows(dest_ref, *refs):
    out_ref = refs[-1]
    base = 0
    for ref in refs[:-1]:
        rows = ref.shape[0]

        def body(s, carry, ref=ref, base=base):
            out_ref[pl.ds(dest_ref[base + s], 1), :] = ref[pl.ds(s, 1), :]
            return carry

        lax.fori_loop(0, rows, body, 0, unroll=8)
        base += rows


def solution(mesh):
    n_idx, n_tp = mesh.shape["idx"], mesh.shape["tp"]
    n_x = n_tp // 2
    n_y = 2 if n_idx % 2 == 0 else 1
    n_z = n_idx // n_y
    fast_gather = n_x == 2 and n_y == 2 and n_z == 4

    def pattern(move):
        pairs = []
        for g in range(n_idx):
            for x in range(n_x):
                for c in range(2):
                    to = move(g, x, c)
                    if to is not None and 0 <= to[0] < n_idx:
                        pairs.append(((g * n_x + x) * 2 + c, (to[0] * n_x + to[1]) * 2 + to[2]))
        return pairs

    to_core = pattern(lambda g, x, c: (g, x, 1 - c))
    to_next = pattern(lambda g, x, c: (g + 1, x, 0) if c == 1 else (g - 1, x, 1))
    ring = pattern(lambda g, x, c: ((g + 1) % n_idx, x, c))
    to_y = pattern(lambda g, x, c: (g ^ 1, x, c))
    z_up = pattern(lambda g, x, c: ((g + n_y) % n_idx, x, c))
    z_down = pattern(lambda g, x, c: ((g - n_y) % n_idx, x, c))

    def to_x(step):
        return pattern(lambda g, x, c: (g, x ^ step, c))

    steps = []
    step = n_x // 2
    while step >= 1:
        steps.append(step)
        step //= 2

    def send(value, pairs):
        return lax.ppermute(value, AXES, pairs)

    def cut(value, index, size, axis):
        return lax.dynamic_slice_in_dim(value, index * size, size, axis)

    def per_device(
        activations, out_grads, proj_in, proj_out, doc_ids, doc_order, inv_fisher, index_grads
    ):
        g, tp = lax.axis_index("idx"), lax.axis_index("tp")
        x, core = tp // 2, tp % 2
        rank = proj_in.shape[1]
        lead = rank // n_tp
        tokens = activations.shape[0]
        half = tokens // 2
        documents = doc_order.shape[0]
        own_docs = documents // n_idx
        piece = own_docs // n_tp

        part = jnp.concatenate(
            [
                jnp.dot(activations, proj_in, preferred_element_type=jnp.float32),
                jnp.dot(out_grads, proj_out, preferred_element_type=jnp.float32),
            ],
            axis=1,
        )
        mine = cut(part, core, half, 0) + send(cut(part, 1 - core, half, 0), to_core)
        acts, grads = mine[:, :rank], mine[:, rank:]
        for step in steps:
            bit = (x // step) % 2
            width = grads.shape[1] // 2
            more_acts = send(acts, to_x(step))
            more_grads = send(cut(grads, 1 - bit, width, 1), to_x(step))
            acts = acts + more_acts
            grads = cut(grads, bit, width, 1) + more_grads

        ids = cut(doc_ids, core, half, 0)
        acts = jnp.concatenate([send(acts, to_next), acts])
        grads = jnp.concatenate([send(grads, to_next), grads])
        ids = jnp.concatenate([send(ids, to_next), ids])
        acts = jnp.concatenate([acts, send(acts, to_core)])
        grads = jnp.concatenate(
            [cut(grads, core, lead, 1), send(cut(grads, 1 - core, lead, 1), to_core)]
        )
        ids = jnp.concatenate([ids, send(ids, to_core)])

        def doc_sums(acts, grads, ids):
            token_grads = (grads[:, :, None] * acts[:, None, :]).reshape(-1, lead * rank)
            own = g * own_docs + jnp.arange(own_docs, dtype=jnp.int32)
            membership = (ids[:, None] == own[None, :]).astype(jnp.float32)
            return lax.dot_general(
                membership,
                token_grads,
                (((0,), (0,)), ((), ())),
                precision=HIGHEST,
                preferred_element_type=jnp.float32,
            )

        group = doc_ids // own_docs
        far = (
            (group[0] < g - 1) | (group[half - 1] > g) | (group[half] < g) | (group[-1] > g + 1)
        )
        far = jnp.broadcast_to(far.astype(jnp.int32), (8, 128))

        def own_queries(doc_grads):
            partial = jnp.dot(
                doc_grads, inv_fisher, precision=HIGH, preferred_element_type=jnp.float32
            )
            rows = own_docs // 2
            partial = cut(partial, core, rows, 0) + send(cut(partial, 1 - core, rows, 0), to_core)
            for step in steps:
                bit = (x // step) % 2
                rows //= 2
                partial = cut(partial, bit, rows, 0) + send(
                    cut(partial, 1 - bit, rows, 0), to_x(step)
                )
            return partial.astype(jnp.bfloat16)

        def first_doc(g, x, c):
            return g * own_docs + c * (own_docs // 2) + x * piece

        def gather(q, far):
            line = jnp.arange(piece, dtype=jnp.int32)
            if not fast_gather:
                everything = lax.all_gather(q, AXES, axis=0, tiled=True)
                where = jnp.concatenate(
                    [
                        first_doc(h, t // 2, t % 2) + line
                        for h in range(n_idx)
                        for t in range(n_tp)
                    ]
                )
                return [everything], where, lax.pmax(far, AXES)
            to_x1 = to_x(1)
            cutoff = piece // 2

            def corner(from_x, from_y):
                return [send(from_y[:cutoff], to_x1), send(from_x[cutoff:], to_y)]

            below, above = send(q, z_up), send(q, z_down)
            far_below, far_above = send(far, z_up), send(far, z_down)
            x0, y0 = send(q, to_x1), send(q, to_y)
            d0 = corner(x0, y0)
            beyond, far_beyond = send(below, z_up), send(far_below, z_up)
            far = far | far_below | far_above | far_beyond
            xb, xa = send(below, to_x1), send(above, to_x1)
            yb, ya = send(below, to_y), send(above, to_y)
            x2, y2 = send(beyond, to_x1), send(beyond, to_y)
            far = far | send(far, to_y)
            db, da = corner(xb, yb), corner(xa, ya)
            d2 = corner(x2, y2)
            batches = [
                jnp.concatenate([q, x0, y0] + d0),
                jnp.concatenate([below, xb, yb] + db + [above, xa, ya] + da),
                jnp.concatenate([beyond, x2, y2] + d2),
            ]
            batches = [jnp.concatenate([b, send(b, to_core)]) for b in batches]

            def docs_of(level, c):
                there = (g + level * n_y) % n_idx
                return [
                    first_doc(h, xx, c) + line
                    for h, xx in ((there, x), (there, 1 - x), (there ^ 1, x), (there ^ 1, 1 - x))
                ]

            where = []
            for levels in ((0,), (-1, 1), (2,)):
                for c in (core, 1 - core):
                    for level in levels:
                        where += docs_of(level, c)
            return batches, jnp.concatenate(where), far

        def place(batches, where):
            rank_of = jnp.sum(
                jnp.where(
                    where[:, None] == doc_order[None, :],
                    jnp.arange(documents, dtype=jnp.int32)[None, :],
                    0,
                ),
                axis=1,
            )
            scores = [
                lax.dot_general(
                    b, index_grads, (((1,), (1,)), ((), ())), preferred_element_type=jnp.float32
                )
                for b in batches
            ]
            columns = index_grads.shape[0]
            return pl.pallas_call(
                place_rows,
                out_shape=jax.ShapeDtypeStruct((documents, columns), jnp.float32),
                in_specs=[pl.BlockSpec(memory_space=pltpu.SMEM)]
                + [pl.BlockSpec(memory_space=pltpu.VMEM)] * len(scores),
                out_specs=pl.BlockSpec(memory_space=pltpu.VMEM),
                compiler_params=pltpu.CompilerParams(vmem_limit_bytes=32 * 1024 * 1024),
            )(rank_of, *scores)

        def near(_):
            return place(batches, where)

        def everywhere(_):
            block = [
                jnp.concatenate([v[half:tokens], v[tokens + half :]]) for v in (acts, grads, ids)
            ]
            total = doc_sums(*block)

            def body(_, carry):
                block, total = carry
                block = [send(v, ring) for v in block]
                return block, total + doc_sums(*block)

            _, total = lax.fori_loop(0, n_idx - 1, body, (block, total))
            batches, where, _ = gather(own_queries(total), far)
            return place(batches, where)

        batches, where, any_far = gather(own_queries(doc_sums(acts, grads, ids)), far)
        return lax.cond(any_far[0, 0] > 0, everywhere, near, 0)

    placed = (
        P("idx", "tp"),
        P("idx", "tp"),
        P("tp", None),
        P("tp", None),
        P("idx"),
        P(),
        P("tp", None),
        P(("idx", "tp"), None),
    )
    return jax.shard_map(
        per_device, mesh=mesh, in_specs=placed, out_specs=P(None, ("idx", "tp")), check_vma=False
    )
```

```python
import functools

import jax
import jax.numpy as jnp
from jax import lax
from jax.experimental import pallas as pl
from jax.experimental.pallas import tpu as pltpu
from jax.sharding import PartitionSpec as P

AXES = ("idx", "tp")
F32, BF16 = jnp.float32, jnp.bfloat16
MIB = 1024 * 1024
IN_SMEM = pl.BlockSpec(memory_space=pltpu.SMEM)
IN_VMEM = pl.BlockSpec(memory_space=pltpu.VMEM)


def across(a, b):
    return lax.dot_general(a, b, (((1,), (1,)), ((), ())), preferred_element_type=F32)


def project(core_ref, acts_ref, grads_ref, in_ref, out_ref, keep_ref, send_ref):
    step = pl.program_id(0)
    rank, tokens = in_ref.shape[0], acts_ref.shape[0]
    blocks = keep_ref.shape[1] // tokens
    place = pl.ds(pl.multiple_of(lax.rem(step, blocks) * tokens, tokens), tokens)
    acts = across(acts_ref[...], in_ref[...]).T
    grads = across(grads_ref[...], out_ref[...]).T
    mine = step // blocks == core_ref[0]

    @pl.when(mine)
    def _():
        keep_ref[:rank, place] = acts
        keep_ref[rank:, place] = grads

    @pl.when(jnp.logical_not(mine))
    def _():
        send_ref[:rank, place] = acts
        send_ref[rank:, place] = grads


def split(value):
    high = value.astype(BF16)
    return high, (value - high.astype(F32)).astype(BF16)


def condition(parts, lead, first_ref, *refs):
    parts_refs = refs[:parts]
    fisher_ref, keep_ref, send_ref, fisher, sums, arrived = refs[parts:]
    blocks, depth, width = fisher.shape

    def fetch(b):
        return pltpu.make_async_copy(
            fisher_ref.at[:, pl.ds(b * width, width)], fisher.at[b], arrived.at[b]
        )

    for b in range(blocks):
        fetch(b).start()
    documents = sums.shape[0] // 2
    rank, tokens = sums.shape[1] // lead, parts_refs[0].shape[1]
    core = first_ref[1]
    own = (first_ref[0] + lax.broadcasted_iota(jnp.int32, (documents, tokens), 0)).astype(F32)
    last = rank + 2 * lead
    members = [(own == ref[last : last + 1, :]).astype(F32).astype(BF16) for ref in parts_refs]
    leads = [
        jnp.where(core == 0, ref[rank : rank + lead, :], ref[rank + lead : last, :])
        for ref in parts_refs
    ]
    for i in range(0, lead, 2):
        total = None
        for member, ref, grads in zip(members, parts_refs, leads, strict=True):
            acts = ref[:rank, :]
            value = jnp.concatenate([grads[i : i + 1, :] * acts, grads[i + 1 : i + 2, :] * acts])
            high, low = split(value)
            term = across(member, high) + across(member, low)
            total = term if total is None else total + term
        high, low = split(total)
        sums[:documents, i * rank : (i + 2) * rank] = high
        sums[documents:, i * rank : (i + 2) * rank] = low
    rows = documents // 2
    for b in range(blocks):
        fetch(b).wait()
        high, low = split(fisher[b])
        both = jnp.dot(sums[...], high, preferred_element_type=F32)
        value = both[:documents] + both[documents:] + jnp.dot(
            sums[:documents, :], low, preferred_element_type=F32
        )
        columns = slice(b * width, (b + 1) * width)
        keep_ref[:, columns] = jnp.where(core == 0, value[:rows], value[rows:])
        send_ref[:, columns] = jnp.where(core == 0, value[rows:], value[:rows])


def score(pieces, *refs):
    index_ref, out_ref, stacked = refs[pieces:]
    base = 0
    for ref in refs[:pieces]:
        stacked[base : base + ref.shape[0], :] = ref[...]
        base += ref.shape[0]
    columns = out_ref.shape[1]
    block = min(256, columns)
    for c in range(0, columns, block):
        out_ref[:, c : c + block] = across(stacked[...], index_ref[c : c + block, :])


def place_rows(dest_ref, *refs):
    out_ref = refs[-1]
    base = 0
    for ref in refs[:-1]:

        def body(group, carry, ref=ref, base=base):
            start = group * 8
            rows = [ref[pl.ds(start + k, 1), :] for k in range(8)]
            for k, row in enumerate(rows):
                out_ref[pl.ds(dest_ref[base + start + k], 1), :] = row
            return carry

        lax.fori_loop(0, ref.shape[0] // 8, body, 0)
        base += ref.shape[0]


def solution(mesh):
    n_idx, n_tp = mesh.shape["idx"], mesh.shape["tp"]
    n_x = n_tp // 2
    n_y = 2 if n_idx % 2 == 0 else 1
    n_z = n_idx // n_y
    box = n_x == 2 and n_y == 2 and n_z == 4

    def pattern(move):
        pairs = []
        for g in range(n_idx):
            for x in range(n_x):
                for c in range(2):
                    to = move(g, x, c)
                    if 0 <= to[0] < n_idx:
                        pairs.append(((g * n_x + x) * 2 + c, (to[0] * n_x + to[1]) * 2 + to[2]))
        return pairs

    to_core = pattern(lambda g, x, c: (g, x, 1 - c))
    to_next = pattern(lambda g, x, c: (g + 1, x, 0) if c == 1 else (g - 1, x, 1))
    ring = pattern(lambda g, x, c: ((g + 1) % n_idx, x, c))
    to_plane = pattern(lambda g, x, c: (g, x ^ 1, c) if c == 0 else (g ^ 1, x, c))
    to_line = pattern(lambda g, x, c: ((g + n_y * (1 - 2 * c)) % n_idx, x, c))

    def to_x(step):
        return pattern(lambda g, x, c: (g, x ^ step, c))

    steps = []
    step = n_x // 2
    while step >= 1:
        steps.append(step)
        step //= 2

    def send(value, pairs):
        return lax.ppermute(value, AXES, pairs)

    def send_all(values, pairs):
        return [send(v, pairs) for v in values]

    def cut(value, index, size, axis):
        return lax.dynamic_slice_in_dim(value, index * size, size, axis)

    def per_device(
        activations, out_grads, proj_in, proj_out, doc_ids, doc_order, inv_fisher, index_grads
    ):
        g, tp = lax.axis_index("idx"), lax.axis_index("tp")
        x, core = tp // 2, tp % 2
        rank = proj_in.shape[1]
        lead = rank // n_tp
        tokens, hidden = activations.shape
        features = out_grads.shape[1]
        half = tokens // 2
        documents = doc_order.shape[0]
        own_docs = documents // n_idx
        piece = own_docs // n_tp
        depth, width = inv_fisher.shape
        columns = index_grads.shape[0]

        block = min(256, half)
        out_half = jax.ShapeDtypeStruct((2 * rank, half), F32)
        keep, give = pl.pallas_call(
            project,
            grid=(tokens // block,),
            in_specs=[
                IN_SMEM,
                pl.BlockSpec((block, hidden), lambda s: (s, 0)),
                pl.BlockSpec((block, features), lambda s: (s, 0)),
                pl.BlockSpec((rank, hidden), lambda s: (0, 0)),
                pl.BlockSpec((rank, features), lambda s: (0, 0)),
            ],
            out_specs=[pl.BlockSpec((2 * rank, half), lambda s: (0, 0))] * 2,
            out_shape=[out_half, out_half],
            compiler_params=pltpu.CompilerParams(vmem_limit_bytes=58 * MIB),
        )(core[None], activations, out_grads, proj_in.T, proj_out.T)
        mine = keep + send(give, to_core)
        for step in steps:
            bit = (x // step) % 2
            rows = (mine.shape[0] - rank) // 2

            def half_of(b, mine=mine, rows=rows):
                return jnp.concatenate([mine[:rank], cut(mine[rank:], b, rows, 0)])

            mine = half_of(bit) + send(half_of(1 - bit), to_x(step))

        ids = jnp.broadcast_to(cut(doc_ids, core, half, 0).astype(F32)[None], (8, half))
        own_part = jnp.concatenate([mine, ids])
        parts = [own_part, send(own_part, to_next)]
        parts += send_all(parts, to_core)

        group = doc_ids // own_docs
        far = (
            (group[0] < g - 1) | (group[half - 1] > g) | (group[half] < g) | (group[-1] > g + 1)
        )

        def conditioned(parts):
            blocks = 8
            out_half = jax.ShapeDtypeStruct((own_docs // 2, width), F32)
            return pl.pallas_call(
                functools.partial(condition, len(parts), lead),
                in_specs=[IN_SMEM]
                + [IN_VMEM] * len(parts)
                + [pl.BlockSpec(memory_space=pl.ANY)],
                out_specs=[IN_VMEM] * 2,
                out_shape=[out_half, out_half],
                scratch_shapes=[
                    pltpu.VMEM((blocks, depth, width // blocks), F32),
                    pltpu.VMEM((2 * own_docs, depth), BF16),
                    pltpu.SemaphoreType.DMA((blocks,)),
                ],
                compiler_params=pltpu.CompilerParams(vmem_limit_bytes=40 * MIB),
            )(
                jnp.stack([g * own_docs, core]),
                *parts,
                inv_fisher,
            )

        def exchange(value, pairs):
            scale = jnp.max(jnp.abs(value), axis=1, keepdims=True)
            scale = jnp.where(scale > 0, scale, 1.0)
            there = send((value / scale).astype(jnp.float16), pairs)
            scale = send(jnp.broadcast_to(scale, (value.shape[0], 128)), pairs)
            return there.astype(F32) * scale[:, :1]

        def own_queries(keep, give):
            partial = keep + send(give, to_core)
            rows = own_docs // 2
            for step in steps:
                bit = (x // step) % 2
                rows //= 2
                partial = cut(partial, bit, rows, 0) + exchange(
                    cut(partial, 1 - bit, rows, 0), to_x(step)
                )
            return partial

        def gather(q):
            if not box:
                everything = lax.all_gather(q, AXES, axis=0, tiled=True)
                origin = [(h, t // 2, t % 2) for h in range(n_idx) for t in range(n_tp)]
                return [[everything]], origin, [everything[h * own_docs :] for h in range(n_idx)]
            own = [q, send(q, to_core)]
            line = send_all(own, to_line)
            plane0 = send_all(own, to_plane)
            other0 = send_all(plane0, to_core)
            corner0 = [send(other0[1], to_plane)]
            corner0 += send_all(corner0, to_core)
            two = [send(line[0], to_line)]
            off = send_all(line, to_core)
            plane1 = send_all(line, to_plane)
            two += send_all(two, to_core)
            plane2 = send_all(off, to_plane)
            corner1 = send_all(corner0, to_line)
            plane3 = send_all(two, to_plane)
            other1, other2 = send_all(plane1, to_core), send_all(plane2, to_core)
            corner3 = [send(corner1[0], to_line)]
            corner2 = send_all(corner1, to_core)
            other3 = send_all(plane3, to_core)
            corner3 += send_all(corner3, to_core)

            there = 1 - 2 * core
            below, above, opposite = [(g + d * n_y) % n_idx for d in (-there, there, 2)]
            mates = ((x ^ 1, 0), (x, 1))
            near_x, near_y = [jnp.where(core == 0, mates[0][i], mates[1][i]) for i in (0, 1)]
            far_x, far_y = [jnp.where(core == 0, mates[1][i], mates[0][i]) for i in (0, 1)]

            def level(h, swapped):
                here = [core, 1 - core]
                near_labels = here[::-1] if swapped else here
                other_labels = here[::-1]
                return (
                    [(h, x, c) for c in near_labels]
                    + [(h ^ near_y, near_x, c) for c in near_labels]
                    + [(h ^ far_y, far_x, c) for c in other_labels[:: -1 if swapped else 1]]
                    + [(h ^ 1, x ^ 1, c) for c in near_labels]
                )

            batches = [
                own + plane0 + other0 + corner0,
                line + plane1 + other2 + corner1,
                off + plane2 + other1 + corner2,
                two + plane3 + other3 + corner3,
            ]
            origin = level(g, False)
            line_level, off_level = level(below, False), level(above, True)
            line_level[4:6], off_level[4:6] = (
                [(h, xx, c) for (h, xx, _), c in zip(line_level[4:6], (core, 1 - core))],
                [(h, xx, c) for (h, xx, _), c in zip(off_level[4:6], (1 - core, core))],
            )
            return batches, origin + line_level + off_level + level(opposite, False), [
                p[0] for p in (own, line, off, two, corner0, corner1, corner2, corner3)
            ]

        def scores_of(batch):
            pieces = len(batch)
            rows = sum(b.shape[0] for b in batch)
            block = min(256, columns)
            return pl.pallas_call(
                functools.partial(score, pieces),
                in_specs=[IN_VMEM] * (pieces + 1),
                out_specs=IN_VMEM,
                out_shape=jax.ShapeDtypeStruct((rows, columns), F32),
                scratch_shapes=[pltpu.VMEM((rows, width), BF16)],
                compiler_params=pltpu.CompilerParams(vmem_limit_bytes=24 * MIB),
                cost_estimate=pl.CostEstimate(
                    flops=2 * rows * columns * width,
                    bytes_accessed=2 * width * columns + 4 * rows * columns,
                    transcendentals=0,
                ),
            )(*batch, index_grads)

        def place(scores, dest):
            return pl.pallas_call(
                place_rows,
                out_shape=jax.ShapeDtypeStruct((documents, columns), F32),
                in_specs=[IN_SMEM] + [IN_VMEM] * len(scores),
                out_specs=IN_VMEM,
                compiler_params=pltpu.CompilerParams(vmem_limit_bytes=32 * MIB),
            )(dest, *scores)

        def rows_of(origin):
            first = jnp.stack([h * own_docs + c * (own_docs // 2) + xx * piece for h, xx, c in origin])
            docs = (first[:, None] + jnp.arange(piece, dtype=jnp.int32)[None, :]).reshape(-1)
            order = jnp.arange(documents, dtype=jnp.int32)[None, :]
            return jnp.sum(jnp.where(docs[:, None] == doc_order[None, :], order, 0), axis=1)

        q = own_queries(*conditioned(parts))
        batches, origin, seen = gather(jnp.where(far, jnp.nan, q).astype(BF16))
        probe = functools.reduce(jnp.add, [p[:8, :128].astype(F32) for p in seen])
        any_far = jnp.isnan(probe[0, 0])
        dest = rows_of(origin)
        scores = [scores_of(b) for b in batches]

        def near(_):
            return place(scores, dest)

        def everywhere(_):
            block = [parts[0], parts[2]]
            total = conditioned(block)

            def body(_, carry):
                block, total = carry
                block = send_all(block, ring)
                return block, [a + b for a, b in zip(total, conditioned(block))]

            _, total = lax.fori_loop(0, n_idx - 1, body, (block, list(total)))
            batches, _, _ = gather(own_queries(*total).astype(BF16))
            return place([scores_of(b) for b in batches], dest)

        return lax.cond(any_far, everywhere, near, 0)

    placed = (
        P("idx", "tp"),
        P("idx", "tp"),
        P("tp", None),
        P("tp", None),
        P("idx"),
        P(),
        P("tp", None),
        P(("idx", "tp"), None),
    )
    return jax.shard_map(
        per_device, mesh=mesh, in_specs=placed, out_specs=P(None, ("idx", "tp")), check_vma=False
    )
```
